256 devices in a mesh: gx: 32 (over x, z), gy: 4 (over y), gz: 2 (over core).
Axes of the slice: x: 4, y: 4, z: 8, core: 2. Of those that a mesh axis runs over, the one named last changes fastest.
Arguments:
- features: float32 [32, 4, 2, 64, 6144], P('gx', 'gy', 'gz'), may hold values from -6 to 6
- boundary_rows: int32 [32, 4, 2, 512], P('gx', 'gy', 'gz'), may hold values from 0 to 6143
- in_maps: int32 [32, 4, 2, 26, 3072], P('gx', 'gy', 'gz'), may hold values from 0 to 19968, as said below
- out_maps: int32 [32, 4, 2, 26, 3072], P('gx', 'gy', 'gz'), may hold values from 0 to 6144, as said below
- send_rows: int32 [32, 4, 2, 32, 384], P('gx', 'gy', 'gz'), may hold values from 0 to 6144, as said below
- recv_coarse: int32 [32, 4, 2, 32, 384], P('gx', 'gy', 'gz'), may hold values from 0 to 3072, as said below
- conv_weight: float32 [27, 64, 64], replicated, may hold values from -0.25 to 0.25
- scale_one: float32 [64], replicated, may hold values from 0.1 to 1.9
- shift_one: float32 [64], replicated, may hold values from -3 to 3
- down_weight: float32 [8, 128, 64], replicated, may hold values from -0.5 to 0.5
- scale_two: float32 [128], replicated, may hold values from 0.1 to 1.9
- shift_two: float32 [128], replicated, may hold values from -3 to 3
Outputs:
- fine_out: float32 [32, 4, 2, 64, 6144], P('gx', 'gy', 'gz')
- coarse_out: float32 [32, 4, 2, 128, 3072], P('gx', 'gy', 'gz')
The draws below stay inside these ranges and needn't reach their ends.
Inputs may be any that keep to these rules, and one draw needn't show every extreme that they name: `in_maps`: live entries of a list come first; each names a column of that block's source table: an own row below 6144, or row r of the buffer of a neighbour in position q at 6144 + q * 512 + r, where q's displacement in each dimension is 0 or that of the list's offset and not all 0. Padding entries name the zero column 19968. Every list has 768 or more live entries, and in every draw some lists are full. `out_maps`: live entries of one list name distinct rows of the block and come first, in the same slots as the live entries of in_maps; padding entries are 6144. `send_rows`: each fine row of a block stands in exactly one slot of that block's table; empty slots hold 6144. In every draw each block fills all 384 slots of some owner. `recv_coarse`: entry [s, t] of owner (a, b, c) is 3072 exactly where send_rows of block (s, b, c) holds 6144 for owner a in slot t, else a coarse row below 3072.
All inputs are finite; a program needn't handle non-finite values.
Results may differ from the reference program's by a relative error of at most 0.0003.
Values sent between devices are 32-bit elements; how exact they have to be, the bound alone decides.
No kernel may reach another device: no remote copies, remote signals or barrier semaphores. Data moves between devices by JAX's collectives and lax.ppermute only.
A program may use at most 64 MiB of HBM per device.

```python
import jax
import jax.numpy as jnp
import numpy as np
from jax import lax

CH = 64
CHO = 128
VOX = 6144
PAIRS = 3072
BND = 512
COARSE = 3072
CAP = 384
N_GX = 32
N_GY = 4
N_GZ = 2


def kernel_lists(key):
    count = N_GX * N_GY * N_GZ
    k_load, k_pick, k_len, k_perm, k_bits, k_local, k_own, k_buf = jax.random.split(key, 8)
    load = jax.random.randint(k_load, (count,), 1, 5)
    heavy = jax.random.randint(k_pick, (), 0, count)
    load = jnp.where(jnp.arange(count) == heavy, 4, load)
    extra = jax.random.randint(k_len, (count, 26), 0, PAIRS // 4)
    live = jnp.where(load[:, None] == 4, PAIRS, jnp.minimum(PAIRS, PAIRS * load[:, None] // 4 + extra))
    alive = jnp.arange(PAIRS)[None, None, :] < live[:, :, None]
    keys = jax.random.split(k_perm, count * 26)
    perms = jax.vmap(lambda k: jax.random.permutation(k, VOX)[:PAIRS])(keys).reshape(count, 26, PAIRS)
    out_maps = jnp.where(alive, perms, VOX)
    offs = np.array([k for k in range(27) if k != 13])
    disp = jnp.asarray(np.stack([offs // 9 - 1, offs // 3 % 3 - 1, offs % 3 - 1], axis=1))
    bits = jax.random.randint(k_bits, (count, 26, PAIRS), 0, 8)
    ex = disp[None, :, None, 0] * (bits // 4)
    ey = disp[None, :, None, 1] * (bits // 2 % 2)
    ez = disp[None, :, None, 2] * (bits % 2)
    empty = (ex == 0) & (ey == 0) & (ez == 0)
    ex = jnp.where(empty, disp[None, :, None, 0], ex)
    ey = jnp.where(empty, disp[None, :, None, 1], ey)
    ez = jnp.where(empty, disp[None, :, None, 2], ez)
    region = (ex + 1) * 9 + (ey + 1) * 3 + (ez + 1)
    local = jax.random.randint(k_local, (count, 26, PAIRS), 0, 2) == 0
    own_row = jax.random.randint(k_own, (count, 26, PAIRS), 0, VOX)
    buf_row = jax.random.randint(k_buf, (count, 26, PAIRS), 0, BND)
    in_maps = jnp.where(local, own_row, VOX + region * BND + buf_row)
    in_maps = jnp.where(alive, in_maps, VOX + 27 * BND)
    shape = (N_GX, N_GY, N_GZ, 26, PAIRS)
    return (in_maps.reshape(shape).astype(jnp.int32), out_maps.reshape(shape).astype(jnp.int32))


def coarse_routes(key):
    count = N_GX * N_GY * N_GZ
    slots = N_GX * CAP

    def one(k):
        k_score, k_full, k_rows = jax.random.split(k, 3)
        idx = jnp.arange(slots, dtype=jnp.int32)
        score = jax.random.randint(k_score, (slots,), 0, 2 ** 14) * slots + idx
        full = jax.random.randint(k_full, (), 0, N_GX)
        score = jnp.where(idx // CAP == full, 2 ** 30 + idx, score)
        unused, chosen = lax.top_k(score, VOX)
        rows = jax.random.permutation(k_rows, VOX).astype(jnp.int32)
        return jnp.full((slots,), VOX, jnp.int32).at[chosen].set(rows)
    table = jax.vmap(one)(jax.random.split(key, count))
    return table.reshape(N_GX, N_GY, N_GZ, N_GX, CAP)


def draw_in_maps(key, part):
    return kernel_lists(key)[0]


def draw_out_maps(key, part):
    return kernel_lists(key)[1]


def draw_send_rows(key, part):
    return coarse_routes(key)


def draw_recv_coarse(key, part):
    table = coarse_routes(key)
    key = jax.random.fold_in(key, 7)
    live = jnp.transpose(table != VOX, (3, 1, 2, 0, 4))
    cols = jax.random.randint(key, live.shape, 0, COARSE)
    return jnp.where(live, cols, COARSE).astype(jnp.int32)


def touch_ends(values, rng, low, top_value):
    place = [jax.random.randint(jax.random.fold_in(rng, axis), (), 0, length) for axis, length in enumerate(values.shape)]
    longest = values.shape.index(max(values.shape))
    beside = place[:longest] + [(place[longest] + 1) % values.shape[longest]] + place[longest + 1:]
    return values.at[tuple(place)].set(low).at[tuple(beside)].set(top_value)


def steps_of(key, extent, cuts, low, high):
    def one(axis_at, parts):
        heights = jax.random.uniform(jax.random.fold_in(jax.random.fold_in(key, 6), axis_at), (parts,), jnp.float32, low / len(cuts), high / len(cuts))
        return jnp.repeat(jnp.exp(heights), extent[axis_at] // parts).reshape((-1,) + (1,) * (len(extent) - axis_at - 1))

    level = one(*cuts[0])
    for cut in cuts[1:]:
        level = level * one(*cut)
    return level


def noise(stream_key, extent, scale, reach, pieces=(), kind=jnp.bfloat16):
    loudness = steps_of(stream_key, extent, pieces, -0.22, 0.18) if pieces else 1.0
    drawn = jax.random.normal(stream_key, extent, jnp.float32) * scale * loudness
    return jnp.minimum(jnp.maximum(drawn, -reach), reach).astype(kind)


def setup_inputs(seed: int = 0) -> dict:
    streams_of = jax.random.split(jax.random.key(seed), 13)
    features = noise(streams_of[0], (N_GX, N_GY, N_GZ, CH, VOX), 1.0, 6.0, ((0, 32), (1, 4), (2, 2)), jnp.float32)
    boundary_rows = touch_ends(jax.random.randint(streams_of[1], (N_GX, N_GY, N_GZ, BND), 0, VOX), jax.random.fold_in(streams_of[1], 1), 0, VOX - 1).astype(jnp.int32)
    in_maps = draw_in_maps(jax.random.fold_in(streams_of[12], 71), 0)
    out_maps = draw_out_maps(jax.random.fold_in(streams_of[12], 71), 0)
    send_rows = draw_send_rows(jax.random.fold_in(streams_of[12], 71), 0)
    recv_coarse = draw_recv_coarse(jax.random.fold_in(streams_of[12], 71), 0)
    conv_weight = noise(streams_of[6], (27, CH, CH), (CH * 9) ** -0.5, 0.25, (), jnp.float32)
    scale_one = jnp.clip(1.0 + 0.18 * jax.random.normal(streams_of[7], (CH,), jnp.float32), 0.1, 1.9)
    shift_one = noise(streams_of[8], (CH,), 0.5, 3.0, (), jnp.float32)
    down_weight = noise(streams_of[9], (8, CHO, CH), (CH * 2) ** -0.5, 0.5, (), jnp.float32)
    scale_two = jnp.clip(1.0 + 0.18 * jax.random.normal(streams_of[10], (CHO,), jnp.float32), 0.1, 1.9)
    shift_two = noise(streams_of[11], (CHO,), 0.5, 3.0, (), jnp.float32)
    return dict(features=features, boundary_rows=boundary_rows, in_maps=in_maps, out_maps=out_maps, send_rows=send_rows, recv_coarse=recv_coarse, conv_weight=conv_weight, scale_one=scale_one, shift_one=shift_one, down_weight=down_weight, scale_two=scale_two, shift_two=shift_two)


HIGH = lax.Precision.HIGHEST


def layer_one(own, near, ins, outs, conv_weight, scale_one, shift_one):
    chans = own.shape[0]
    source = jnp.concatenate([own, near, jnp.zeros((chans, 1), jnp.float32)], axis=1)
    centre = jnp.dot(conv_weight[13], own, precision=HIGH)
    total = jnp.concatenate([centre, jnp.zeros((chans, 1), jnp.float32)], axis=1)
    others = jnp.concatenate([conv_weight[:13], conv_weight[14:]], axis=0)

    def step(acc, item):
        weight, src_cols, dst_cols = item
        picked = jnp.take(source, src_cols, axis=1)
        return acc.at[:, dst_cols].add(jnp.dot(weight, picked, precision=HIGH)), None

    total, unused = lax.scan(step, total, (others, ins, outs))
    return jnp.maximum(scale_one[:, None] * total[:, :VOX] + shift_one[:, None], 0.0)


def reference(features, boundary_rows, in_maps, out_maps, send_rows, recv_coarse, conv_weight, scale_one, shift_one, down_weight, scale_two, shift_two):
    ngx, ngy, ngz = N_GX, N_GY, N_GZ
    buffers = jnp.take_along_axis(features, boundary_rows[:, :, :, None, :], axis=4)
    padded = jnp.pad(buffers, ((1, 1), (1, 1), (1, 1), (0, 0), (0, 0)))
    zero = jnp.zeros((), jnp.int32)

    def fine_one(flat):
        first = flat // (ngy * ngz)
        second = (flat // ngz) % ngy
        third = flat % ngz
        near = lax.dynamic_slice(padded, (first, second, third, zero, zero), (3, 3, 3, CH, BND))
        near = jnp.transpose(near, (3, 0, 1, 2, 4)).reshape(CH, 27 * BND)
        return layer_one(features[first, second, third], near, in_maps[first, second, third], out_maps[first, second, third], conv_weight, scale_one, shift_one)

    fine = lax.map(fine_one, jnp.arange(ngx * ngy * ngz, dtype=jnp.int32)).reshape(ngx, ngy, ngz, CH, VOX)
    fine_pad = jnp.pad(fine, ((0, 0), (0, 0), (0, 0), (0, 0), (0, 1)))
    sources = jnp.arange(ngx, dtype=jnp.int32)

    def coarse_one(flat):
        first = flat // (ngy * ngz)
        second = (flat // ngz) % ngy
        third = flat % ngz
        rows = send_rows[:, second, third, first]
        picked = fine_pad[sources[:, None], second, third, :, rows]
        picked = jnp.transpose(picked, (0, 2, 1)).reshape(ngx, CH, 8, CAP // 8)
        part = jnp.einsum("omc,scon->mson", down_weight, picked, precision=HIGH).reshape(CHO, ngx * CAP)
        cols = recv_coarse[first, second, third].reshape(-1)
        total = jnp.zeros((CHO, COARSE + 1), jnp.float32).at[:, cols].add(part)
        return jnp.maximum(scale_two[:, None] * total[:, :COARSE] + shift_two[:, None], 0.0)

    coarse = lax.map(coarse_one, jnp.arange(ngx * ngy * ngz, dtype=jnp.int32)).reshape(ngx, ngy, ngz, CHO, COARSE)
    return fine, coarse
```

```python
import functools

import jax
import jax.numpy as jnp
from jax import lax
from jax.experimental import pallas as pl
from jax.experimental.pallas import tpu as pltpu
from jax.sharding import PartitionSpec as P

CH = 64
CHO = 128
VOX = 6144
PAIRS = 3072
BND = 512
COARSE = 3072
OWNERS = 32
CAP = 384
ZERO_ROW = VOX + 27 * BND
TABLE = ZERO_ROW + 8
ROWS = VOX + 8
TILE = 256
TILES = VOX // TILE
PER_TILE = PAIRS // TILES
STEPS = 13
GROUP = 48
HALF = CAP // 2
ACCS = 8
F32 = jnp.float32
BF16 = jnp.bfloat16
MIB = 1 << 20

VMEM = pl.BlockSpec(memory_space=pltpu.VMEM)
SMEM = pl.BlockSpec(memory_space=pltpu.SMEM)
ANY = pl.BlockSpec(memory_space=pl.ANY)


def params(mib):
    return pltpu.CompilerParams(vmem_limit_bytes=mib * MIB)


def low_lanes(rows=1):
    return lax.broadcasted_iota(jnp.int32, (rows, 128), 1) < CH


def split(x):
    hi = x.astype(BF16)
    lo = (x - hi.astype(F32)).astype(BF16)
    return hi, lo


def prep_kernel(own_ref, rows_ref, table_ref, buf_ref):
    def turn(t, carry):
        at = pl.ds(pl.multiple_of(t * TILE, TILE), TILE)
        x = own_ref[:, at]
        table_ref[at, :] = jnp.concatenate([x, x], axis=0).T
        return carry

    lax.fori_loop(0, TILES, turn, 0)
    low = low_lanes()

    def pick(i, carry):
        for u in range(32):
            r = i * 32 + u
            first = table_ref[pl.ds(rows_ref[0, r], 1), :]
            second = table_ref[pl.ds(rows_ref[0, r + BND // 2], 1), :]
            buf_ref[pl.ds(r, 1), :] = jnp.where(low, first, second)
        return carry

    lax.fori_loop(0, BND // 64, pick, 0)


def prep(own, rows):
    return pl.pallas_call(
        prep_kernel,
        out_shape=(
            jax.ShapeDtypeStruct((VOX, 128), F32),
            jax.ShapeDtypeStruct((BND // 2, 128), F32),
        ),
        in_specs=[VMEM, SMEM],
        out_specs=(VMEM, VMEM),
        compiler_params=params(32),
        name="prep",
    )(own, rows)


def spread(s_ref, start, buf):
    other = pltpu.roll(buf, CH, 1)
    low = low_lanes(BND // 2)
    s_ref[pl.ds(start, BND // 2), :] = jnp.where(low, buf, other)
    s_ref[pl.ds(start + BND // 2, BND // 2), :] = jnp.where(low, other, buf)


def conv_kernel(
    place_ref, own_ref, mid_ref, far_ref, ins_ref, outs_ref, w_ref, scale_ref, shift_ref,
    fine_ref, rows_ref,
    s_ref, g0_ref, g1_ref, acc_ref, in_ref, out_ref, own_sem, cen_sem, in_sem, out_sem,
):
    own_copy = pltpu.make_async_copy(own_ref, s_ref.at[pl.ds(0, VOX), :], own_sem)
    cen_copy = pltpu.make_async_copy(own_ref, g1_ref.at[pl.ds(0, VOX), :], cen_sem)
    own_copy.start()
    cen_copy.start()

    def lists(s, slot):
        return (
            pltpu.make_async_copy(ins_ref.at[pl.ds(2 * s, 2)], in_ref.at[slot], in_sem.at[slot]),
            pltpu.make_async_copy(outs_ref.at[pl.ds(2 * s, 2)], out_ref.at[slot], out_sem.at[slot]),
        )

    for copy in lists(0, 0):
        copy.start()
    here = place_ref[0]
    other = 2 - 2 * here
    same = 2 * here
    empty = jnp.zeros((BND, 128), F32)

    def fill(e, carry):
        base = VOX + e * 3 * BND
        spread(s_ref, pl.multiple_of(base + BND, BND), mid_ref[e])
        spread(s_ref, pl.multiple_of(base + other * BND, BND), far_ref[e])
        s_ref[pl.ds(pl.multiple_of(base + same * BND, BND), BND), :] = empty
        return carry

    lax.fori_loop(0, 9, fill, 0)
    s_ref[pl.ds(ZERO_ROW, 8), :] = jnp.zeros((8, 128), F32)

    def clear(t, carry):
        at = pl.ds(pl.multiple_of(t * TILE, TILE), TILE)
        g0_ref[at, :] = jnp.zeros((TILE, 128), F32)
        acc_ref[at, :] = jnp.zeros((TILE, 128), F32)
        return carry

    lax.fori_loop(0, TILES, clear, 0)
    low = low_lanes()
    high = jnp.logical_not(low)
    own_copy.wait()
    cen_copy.wait()

    def product(ref, at, s):
        hi, lo = split(ref[at, :])
        return jnp.dot(
            jnp.concatenate([hi, lo], axis=1), w_ref[s], preferred_element_type=F32
        )

    def phase(s, slot, now_ref, last_ref, more):
        for copy in lists(s, slot):
            copy.wait()
        if more:
            for copy in lists(s + 1, 1 - slot):
                copy.start()

        def body(t, carry):
            at = pl.ds(pl.multiple_of(t * TILE, TILE), TILE)
            acc_ref[at, :] += product(last_ref, at, s)
            last_ref[at, :] = jnp.zeros((TILE, 128), F32)
            for u in range(PER_TILE):
                p = t * PER_TILE + u
                for j, mask in ((0, low), (1, high)):
                    row = s_ref[pl.ds(in_ref[slot, j, 0, p], 1), :]
                    pltpu.store(
                        now_ref.at[pl.ds(out_ref[slot, j, 0, p], 1), :], row, mask=mask
                    )
            return carry

        lax.fori_loop(0, TILES, body, 0)

    def two(i, carry):
        phase(2 * i, 0, g0_ref, g1_ref, True)
        phase(2 * i + 1, 1, g1_ref, g0_ref, True)
        return carry

    lax.fori_loop(0, (STEPS - 1) // 2, two, 0)
    phase(STEPS - 1, 0, g0_ref, g1_ref, False)
    low_tile = low_lanes(128)

    def finish(t, carry):
        at = pl.ds(pl.multiple_of(t * TILE, TILE), TILE)
        total = acc_ref[at, :] + product(g0_ref, at, STEPS)
        total = total + pltpu.roll(total, CH, 1)
        fine = jnp.maximum(scale_ref[...] * total + shift_ref[...], 0.0)
        rows_ref[at, :] = fine
        turned = jnp.where(low_tile, fine[:128], fine[128:]).T
        fine_ref[:, pl.ds(pl.multiple_of(t * TILE, TILE), 128)] = turned[:CH]
        fine_ref[:, pl.ds(pl.multiple_of(t * TILE + 128, 128), 128)] = turned[CH:]
        return carry

    lax.fori_loop(0, TILES, finish, 0)
    rows_ref[pl.ds(VOX, 8), :] = jnp.zeros((8, 128), F32)


def conv(place, own, mid, far, ins, outs, weights, scale, shift):
    return pl.pallas_call(
        conv_kernel,
        out_shape=(
            jax.ShapeDtypeStruct((CH, VOX), F32),
            jax.ShapeDtypeStruct((ROWS, 128), F32),
        ),
        in_specs=[SMEM, ANY, VMEM, VMEM, ANY, ANY, VMEM, VMEM, VMEM],
        out_specs=(VMEM, VMEM),
        scratch_shapes=[
            pltpu.VMEM((TABLE, 128), F32),
            pltpu.VMEM((ROWS, 128), F32),
            pltpu.VMEM((ROWS, 128), F32),
            pltpu.VMEM((VOX, 128), F32),
            pltpu.SMEM((2, 2, 1, PAIRS), jnp.int32),
            pltpu.SMEM((2, 2, 1, PAIRS), jnp.int32),
            pltpu.SemaphoreType.DMA,
            pltpu.SemaphoreType.DMA,
            pltpu.SemaphoreType.DMA((2,)),
            pltpu.SemaphoreType.DMA((2,)),
        ],
        compiler_params=params(48),
        name="conv",
    )(place, own, mid, far, ins, outs, weights, scale, shift)


def pack_kernel(rows_ref, table_ref, out_ref):
    low = low_lanes()

    def owner(a, carry):
        for r in range(HALF):
            first = rows_ref[pl.ds(table_ref[a, r], 1), :]
            second = rows_ref[pl.ds(table_ref[a, r + HALF], 1), :]
            out_ref[a, pl.ds(r, 1), :] = jnp.where(low, first, second)
        return carry

    lax.fori_loop(0, OWNERS, owner, 0)


def pack(rows, table):
    return pl.pallas_call(
        pack_kernel,
        out_shape=jax.ShapeDtypeStruct((OWNERS, HALF, 128), F32),
        in_specs=[VMEM, SMEM],
        out_specs=VMEM,
        compiler_params=params(32),
        name="pack",
    )(rows, table)


def down_kernel(x_ref, cols_ref, w_ref, scale_ref, shift_ref, out_ref, p0_ref, p1_ref, *z_refs):
    def clear(t, carry):
        at = pl.ds(pl.multiple_of(t * 128, 128), 128)
        for z_ref in z_refs:
            z_ref[at, :] = jnp.zeros((128, 128), F32)
        return carry

    lax.fori_loop(0, COARSE // 128, clear, 0)

    def source(s, carry):
        for c in range(4):
            hi, lo = split(x_ref[s, pl.ds(c * GROUP, GROUP), :])
            part = jnp.dot(hi, w_ref[0, c], preferred_element_type=F32)
            part += jnp.dot(lo, w_ref[0, c], preferred_element_type=F32)
            part += jnp.dot(hi, w_ref[1, c], preferred_element_type=F32)
            p0_ref[pl.ds(c * GROUP, GROUP), :] = part[:, :128]
            p1_ref[pl.ds(c * GROUP, GROUP), :] = part[:, 128:]
        for r in range(0, HALF, ACCS // 2):
            todo = []
            for u in range(ACCS // 2):
                for j, p_ref in enumerate((p0_ref, p1_ref)):
                    at = pl.ds(cols_ref[s, r + u + j * HALF], 1)
                    z_ref = z_refs[2 * u + j]
                    todo.append((z_ref, at, z_ref[at, :] + p_ref[pl.ds(r + u, 1), :]))
            for z_ref, at, value in todo:
                z_ref[at, :] = value
        return carry

    lax.fori_loop(0, OWNERS, source, 0)

    def finish(t, carry):
        at = pl.ds(pl.multiple_of(t * 128, 128), 128)
        total = z_refs[0][at, :]
        for z_ref in z_refs[1:]:
            total = total + z_ref[at, :]
        out_ref[:, at] = jnp.maximum(scale_ref[...] * total + shift_ref[...], 0.0).T
        return carry

    lax.fori_loop(0, COARSE // 128, finish, 0)


def down(arrived, cols, weights, scale, shift):
    return pl.pallas_call(
        down_kernel,
        out_shape=jax.ShapeDtypeStruct((CHO, COARSE), F32),
        in_specs=[VMEM, SMEM, VMEM, VMEM, VMEM],
        out_specs=VMEM,
        scratch_shapes=[pltpu.VMEM((HALF, 128), F32)] * 2
        + [pltpu.VMEM((COARSE + 8, 128), F32)] * ACCS,
        compiler_params=params(48),
        name="down",
    )(arrived, cols, weights, scale, shift)


def neighbours(axis, block):
    count = lax.axis_size(axis)
    forward = [(i, i + 1) for i in range(count - 1)]
    backward = [(target, source) for source, target in forward]
    return lax.ppermute(block, axis, forward), lax.ppermute(block, axis, backward)


def two_parts(w):
    hi = lax.reduce_precision(w, 8, 7)
    return hi.astype(BF16), (w - hi).astype(BF16)


def conv_weights(w):
    hi, lo = two_parts(jnp.swapaxes(w, 1, 2))
    top = jnp.concatenate([hi, lo], axis=2)
    bottom = jnp.concatenate([hi, jnp.zeros_like(hi)], axis=2)

    def arrange(x):
        pairs = jnp.concatenate([x[:13], x[14:]], axis=0).reshape(STEPS, 128, 128)
        centre = jnp.concatenate([x[13], jnp.zeros_like(x[13])], axis=0)
        return jnp.concatenate([centre[None], pairs], axis=0)

    return jnp.concatenate([arrange(top), arrange(bottom)], axis=1)


def down_weights(w):
    turned = jnp.swapaxes(w, 1, 2)
    zero = jnp.zeros_like(turned[:4])
    both = jnp.concatenate(
        [
            jnp.concatenate([turned[:4], zero], axis=2),
            jnp.concatenate([zero, turned[4:]], axis=2),
        ],
        axis=1,
    )
    return jnp.stack(two_parts(both))


def body(
    features,
    boundary_rows,
    in_maps,
    out_maps,
    send_rows,
    recv_coarse,
    conv_weight,
    scale_one,
    shift_one,
    down_weight,
    scale_two,
    shift_two,
):
    own, buf = prep(features[0, 0, 0], boundary_rows[0, 0])
    left, right = neighbours("gx", buf)
    line = jnp.stack([left, buf, right])
    low, high = neighbours("gy", line)
    mid = jnp.stack([low, line, high], axis=1).reshape(9, BND // 2, 128)
    far = lax.ppermute(mid, "gz", [(0, 1), (1, 0)])
    place = lax.axis_index("gz").astype(jnp.int32).reshape(1)
    fine, rows = conv(
        place,
        own,
        mid,
        far,
        in_maps[0, 0, 0].reshape(26, 1, PAIRS),
        out_maps[0, 0, 0].reshape(26, 1, PAIRS),
        conv_weights(conv_weight),
        jnp.tile(scale_one, 2)[None],
        jnp.tile(shift_one, 2)[None],
    )
    packed = pack(rows, send_rows[0, 0, 0])
    arrived = lax.all_to_all(packed, "gx", split_axis=0, concat_axis=0, tiled=True)
    coarse = down(
        arrived,
        recv_coarse[0, 0, 0],
        down_weights(down_weight),
        scale_two[None],
        shift_two[None],
    )
    return (fine[None, None, None], coarse[None, None, None])


def solution(mesh):
    return jax.shard_map(
        body,
        mesh=mesh,
        in_specs=(
            P("gx", "gy", "gz", None, None),
            P("gx", "gy", "gz", None),
            P("gx", "gy", "gz", None, None),
            P("gx", "gy", "gz", None, None),
            P("gx", "gy", "gz", None, None),
            P("gx", "gy", "gz", None, None),
            P(),
            P(),
            P(),
            P(),
            P(),
            P(),
        ),
        out_specs=(P("gx", "gy", "gz", None, None), P("gx", "gy", "gz", None, None)),
        check_vma=False,
    )
```

```python
import functools

import jax
import jax.numpy as jnp
from jax import lax
from jax.experimental import pallas as pl
from jax.experimental.pallas import tpu as pltpu
from jax.sharding import PartitionSpec as P

CH = 64
CHO = 128
VOX = 6144
PAIRS = 3072
BND = 512
COARSE = 3072
OWNERS = 32
CAP = 384
ZERO_ROW = VOX + 27 * BND
TABLE = ZERO_ROW + 8
ROWS = VOX + 8
TILE = 256
TILES = VOX // TILE
BLOCK = 512
BLOCKS = VOX // BLOCK
STEPS = 13
GROUP = 48
HALF = CAP // 2
ACCS = 8
CHUNKS = 2
PART = HALF // CHUNKS
GROUPS = PART // GROUP
F32 = jnp.float32
BF16 = jnp.bfloat16
MIB = 1 << 20

VMEM = pl.BlockSpec(memory_space=pltpu.VMEM)
SMEM = pl.BlockSpec(memory_space=pltpu.SMEM)
ANY = pl.BlockSpec(memory_space=pl.ANY)


def params(mib):
    return pltpu.CompilerParams(vmem_limit_bytes=mib * MIB)


def low_lanes(rows=1):
    return lax.broadcasted_iota(jnp.int32, (rows, 128), 1) < CH


def split(x):
    hi = x.astype(BF16)
    lo = (x - hi.astype(F32)).astype(BF16)
    return hi, lo


def prep_kernel(own_ref, rows_ref, table_ref, buf_ref):
    def turn(t, carry):
        at = pl.ds(pl.multiple_of(t * TILE, TILE), TILE)
        x = own_ref[:, at]
        table_ref[at, :] = jnp.concatenate([x, x], axis=0).T
        return carry

    lax.fori_loop(0, TILES, turn, 0)
    low = low_lanes()

    def pick(i, carry):
        for u in range(32):
            r = i * 32 + u
            first = table_ref[pl.ds(rows_ref[0, r], 1), :]
            second = table_ref[pl.ds(rows_ref[0, r + BND // 2], 1), :]
            buf_ref[pl.ds(r, 1), :] = jnp.where(low, first, second)
        return carry

    lax.fori_loop(0, BND // 64, pick, 0)


def prep(own, rows):
    return pl.pallas_call(
        prep_kernel,
        out_shape=(
            jax.ShapeDtypeStruct((VOX, 128), F32),
            jax.ShapeDtypeStruct((BND // 2, 128), F32),
        ),
        in_specs=[VMEM, SMEM],
        out_specs=(VMEM, VMEM),
        compiler_params=params(32),
        name="prep",
    )(own, rows)


def spread(s_ref, start, buf):
    other = pltpu.roll(buf, CH, 1)
    low = low_lanes(BND // 2)
    s_ref[pl.ds(start, BND // 2), :] = jnp.where(low, buf, other)
    s_ref[pl.ds(start + BND // 2, BND // 2), :] = jnp.where(low, other, buf)


def conv_kernel(
    place_ref, own_ref, mid_ref, far_ref, ins_ref, outs_ref, w_ref, scale_ref, shift_ref,
    fine_ref, rows_ref,
    s_ref, g0_ref, g1_ref, acc_ref, own_sem, cen_sem, list_sem, *list_refs,
):
    own_copy = pltpu.make_async_copy(own_ref, s_ref.at[pl.ds(0, VOX), :], own_sem)
    cen_copy = pltpu.make_async_copy(own_ref, g1_ref.at[pl.ds(0, VOX), :], cen_sem)
    own_copy.start()
    cen_copy.start()

    def lists(s, slot):
        return [
            pltpu.make_async_copy(
                (ins_ref, outs_ref)[i // 4].at[s, i // 2 % 2, i % 2],
                ref.at[slot],
                list_sem.at[slot, i],
            )
            for i, ref in enumerate(list_refs)
        ]

    for copy in lists(0, 0):
        copy.start()
    here = place_ref[0]
    other = 2 - 2 * here
    same = 2 * here
    empty = jnp.zeros((BND, 128), F32)

    def fill(e, carry):
        base = VOX + e * 3 * BND
        spread(s_ref, pl.multiple_of(base + BND, BND), mid_ref[e])
        spread(s_ref, pl.multiple_of(base + other * BND, BND), far_ref[e])
        s_ref[pl.ds(pl.multiple_of(base + same * BND, BND), BND), :] = empty
        return carry

    lax.fori_loop(0, 9, fill, 0)
    s_ref[pl.ds(ZERO_ROW, 8), :] = jnp.zeros((8, 128), F32)

    def clear(t, carry):
        at = pl.ds(pl.multiple_of(t * TILE, TILE), TILE)
        g0_ref[at, :] = jnp.zeros((TILE, 128), F32)
        acc_ref[at, :] = jnp.zeros((TILE, 128), F32)
        return carry

    lax.fori_loop(0, TILES, clear, 0)
    low = low_lanes()
    high = jnp.logical_not(low)
    own_copy.wait()
    cen_copy.wait()

    def product(ref, at, s):
        hi, lo = split(ref[at, :])
        return jnp.dot(
            jnp.concatenate([hi, lo], axis=1), w_ref[s], preferred_element_type=F32
        )

    def phase(s, slot, now_ref, last_ref, more):
        for copy in lists(s, slot):
            copy.wait()
        if more:
            for copy in lists(s + 1, 1 - slot):
                copy.start()

        def body(t, carry):
            at = pl.ds(pl.multiple_of(t * BLOCK, BLOCK), BLOCK)
            acc_ref[at, :] += product(last_ref, at, s)
            last_ref[at, :] = jnp.zeros((BLOCK, 128), F32)
            for u in range(128):
                for i in range(4):
                    row = s_ref[pl.ds(list_refs[i][slot, t, u], 1), :]
                    pltpu.store(
                        now_ref.at[pl.ds(list_refs[i + 4][slot, t, u], 1), :],
                        row,
                        mask=(low, high)[i // 2],
                    )
            return carry

        lax.fori_loop(0, BLOCKS, body, 0)

    def two(i, carry):
        phase(2 * i, 0, g0_ref, g1_ref, True)
        phase(2 * i + 1, 1, g1_ref, g0_ref, True)
        return carry

    lax.fori_loop(0, (STEPS - 1) // 2, two, 0)
    phase(STEPS - 1, 0, g0_ref, g1_ref, False)
    low_tile = low_lanes(128)
    scale, shift = (jnp.concatenate([ref[...]] * 2, axis=1) for ref in (scale_ref, shift_ref))

    def finish(t, carry):
        at = pl.ds(pl.multiple_of(t * TILE, TILE), TILE)
        total = acc_ref[at, :] + product(g0_ref, at, STEPS)
        total = total + pltpu.roll(total, CH, 1)
        fine = jnp.maximum(scale * total + shift, 0.0)
        rows_ref[at, :] = fine
        turned = jnp.where(low_tile, fine[:128], fine[128:]).T
        fine_ref[:, pl.ds(pl.multiple_of(t * TILE, TILE), 128)] = turned[:CH]
        fine_ref[:, pl.ds(pl.multiple_of(t * TILE + 128, 128), 128)] = turned[CH:]
        return carry

    lax.fori_loop(0, TILES, finish, 0)
    rows_ref[pl.ds(VOX, 8), :] = jnp.zeros((8, 128), F32)


def conv(place, own, mid, far, ins, outs, weights, scale, shift):
    return pl.pallas_call(
        conv_kernel,
        out_shape=(
            jax.ShapeDtypeStruct((CH, VOX), F32),
            jax.ShapeDtypeStruct((ROWS, 128), F32),
        ),
        in_specs=[SMEM, ANY, VMEM, VMEM, ANY, ANY, VMEM, VMEM, VMEM],
        out_specs=(VMEM, VMEM),
        scratch_shapes=[
            pltpu.VMEM((TABLE, 128), F32),
            pltpu.VMEM((ROWS, 128), F32),
            pltpu.VMEM((ROWS, 128), F32),
            pltpu.VMEM((VOX, 128), F32),
            pltpu.SemaphoreType.DMA,
            pltpu.SemaphoreType.DMA,
            pltpu.SemaphoreType.DMA((2, 8)),
        ]
        + [pltpu.SMEM((2, BLOCKS, 128), jnp.int32)] * 8,
        compiler_params=params(48),
        name="conv",
    )(place, own, mid, far, ins, outs, weights, scale, shift)


SPLIT = OWNERS // 2
SLOT_SCRATCH = [pltpu.SemaphoreType.DMA((2,))] + [pltpu.SMEM((SPLIT, CAP), jnp.int32)] * 2


def slot_tables(table_ref, sem, refs):
    copies = [
        pltpu.make_async_copy(table_ref.at[pl.ds(i * SPLIT, SPLIT), :], ref, sem.at[i])
        for i, ref in enumerate(refs)
    ]
    for copy in copies:
        copy.start()
    for copy in copies:
        copy.wait()


def pack_kernel(chunk, rows_ref, table_ref, out_ref, sem, *refs):
    slot_tables(table_ref, sem, refs)
    low = low_lanes()

    def owner(a, carry):
        for u in range(PART):
            r = chunk * PART + u
            for half, ref in enumerate(refs):
                first = rows_ref[pl.ds(ref[a, r], 1), :]
                second = rows_ref[pl.ds(ref[a, r + HALF], 1), :]
                out_ref[a + half * SPLIT, pl.ds(u, 1), :] = jnp.where(low, first, second)
        return carry

    lax.fori_loop(0, SPLIT, owner, 0)


def pack(rows, table, chunk):
    return pl.pallas_call(
        functools.partial(pack_kernel, chunk),
        out_shape=jax.ShapeDtypeStruct((OWNERS, PART, 128), F32),
        in_specs=[VMEM, ANY],
        out_specs=VMEM,
        scratch_shapes=SLOT_SCRATCH,
        compiler_params=params(16),
        cost_estimate=pl.CostEstimate(flops=0, bytes_accessed=10 * MIB, transcendentals=0),
        name=f"pack{chunk}",
    )(rows, table)


def down_kernel(chunk, first, last, *args):
    ins, rest = args[: 3 if first else 4], args[3 if first else 4 :]
    x_ref, cols_ref, w_ref = ins[:3]
    if last:
        scale_ref, shift_ref, *rest = rest
    out_ref, sem, c0_ref, c1_ref, p0_ref, p1_ref, *z_refs = rest
    refs = (c0_ref, c1_ref)
    slot_tables(cols_ref, sem, refs)

    def clear(t, carry):
        at = pl.ds(pl.multiple_of(t * 128, 128), 128)
        for z_ref in z_refs:
            z_ref[at, :] = jnp.zeros((128, 128), F32)
        return carry

    lax.fori_loop(0, COARSE // 128, clear, 0)
    for g in range(GROUPS):

        def multiply(i, carry):
            x = x_ref[pl.ds(i * 8, 8), pl.ds(g * GROUP, GROUP), :].reshape(8 * GROUP, 128)
            hi, lo = split(x)
            part = jnp.dot(hi, w_ref[0, chunk * GROUPS + g], preferred_element_type=F32)
            part += jnp.dot(lo, w_ref[0, chunk * GROUPS + g], preferred_element_type=F32)
            part += jnp.dot(hi, w_ref[1, chunk * GROUPS + g], preferred_element_type=F32)
            at = pl.ds(pl.multiple_of((g * OWNERS + i * 8) * GROUP, 8 * GROUP), 8 * GROUP)
            p0_ref[at, :] = part[:, :128]
            p1_ref[at, :] = part[:, 128:]
            return carry

        lax.fori_loop(0, OWNERS // 8, multiply, 0)

    def source(s, carry):
        for u in range(0, PART, ACCS // 4):
            todo = []
            for k in range(ACCS // 4):
                group, place = divmod(u + k, GROUP)
                for i in range(4):
                    row = (group * OWNERS + s + i % 2 * SPLIT) * GROUP + place
                    at = pl.ds(refs[i % 2][s, chunk * PART + u + k + i // 2 * HALF], 1)
                    z_ref = z_refs[4 * k + i]
                    todo.append((z_ref, at, z_ref[at, :] + (p0_ref, p1_ref)[i // 2][pl.ds(row, 1), :]))
            for z_ref, at, value in todo:
                z_ref[at, :] = value
        return carry

    lax.fori_loop(0, SPLIT, source, 0)

    def finish(t, carry):
        at = pl.ds(pl.multiple_of(t * 128, 128), 128)
        total = z_refs[0][at, :]
        for z_ref in z_refs[1:]:
            total = total + z_ref[at, :]
        if not first:
            total = total + ins[3][at, :]
        if last:
            out_ref[:, at] = jnp.maximum(scale_ref[...] * total + shift_ref[...], 0.0).T
        else:
            out_ref[at, :] = total
        return carry

    lax.fori_loop(0, COARSE // 128, finish, 0)


def down(chunk, arrived, cols, weights, before, scale, shift):
    last = chunk == CHUNKS - 1
    operands = [arrived, cols, weights]
    specs = [VMEM, ANY, VMEM]
    if before is not None:
        operands.append(before)
        specs.append(VMEM)
    if last:
        operands += [scale, shift]
        specs += [VMEM, VMEM]
    return pl.pallas_call(
        functools.partial(down_kernel, chunk, before is None, last),
        out_shape=jax.ShapeDtypeStruct((CHO, COARSE) if last else (COARSE, CHO), F32),
        in_specs=specs,
        out_specs=VMEM,
        scratch_shapes=SLOT_SCRATCH
        + [pltpu.VMEM((OWNERS * PART, 128), F32)] * 2
        + [pltpu.VMEM((COARSE + 8, 128), F32)] * ACCS,
        compiler_params=params(40),
        cost_estimate=pl.CostEstimate(flops=0, bytes_accessed=20 * MIB, transcendentals=0),
        name=f"down{chunk}",
    )(*operands)


def neighbours(axis, block):
    count = lax.axis_size(axis)
    forward = [(i, i + 1) for i in range(count - 1)]
    backward = [(target, source) for source, target in forward]
    return lax.ppermute(block, axis, forward), lax.ppermute(block, axis, backward)


def weights_kernel(conv_ref, down_ref, conv_out_ref, down_out_ref):
    empty = jnp.zeros((CH, 128), F32)
    for s in range(STEPS + 1):
        if s == 0:
            first, second = conv_ref[13], jnp.zeros((CH, CH), F32)
        else:
            first, second = (conv_ref[k + (k >= 13)] for k in (2 * s - 2, 2 * s - 1))
        both = jnp.concatenate([first, second], axis=1)
        hi = both.astype(BF16).astype(F32)
        top = jnp.concatenate([hi, both - hi], axis=0)
        bottom = jnp.concatenate([hi, empty], axis=0)
        conv_out_ref[s, :128, :] = top.T.astype(BF16)
        conv_out_ref[s, 128:, :] = bottom.T.astype(BF16)
    left = lax.broadcasted_iota(jnp.int32, (128, CHO), 0) < CH
    for c in range(4):
        both = jnp.concatenate([down_ref[c], down_ref[c + 4]], axis=1).T
        for i, part in enumerate(split(both)):
            part = part.astype(F32)
            down_out_ref[i, c, :, :CHO] = jnp.where(left, part, 0.0).astype(BF16)
            down_out_ref[i, c, :, CHO:] = jnp.where(left, 0.0, part).astype(BF16)


def arrange_weights(conv_weight, down_weight):
    return pl.pallas_call(
        weights_kernel,
        out_shape=(
            jax.ShapeDtypeStruct((STEPS + 1, 256, 128), BF16),
            jax.ShapeDtypeStruct((2, 4, 128, 2 * CHO), BF16),
        ),
        in_specs=[VMEM, VMEM],
        out_specs=(VMEM, VMEM),
        compiler_params=params(16),
        cost_estimate=pl.CostEstimate(flops=0, bytes_accessed=10 * MIB, transcendentals=0),
        name="weights",
    )(conv_weight, down_weight)


def body(
    features,
    boundary_rows,
    in_maps,
    out_maps,
    send_rows,
    recv_coarse,
    conv_weight,
    scale_one,
    shift_one,
    down_weight,
    scale_two,
    shift_two,
):
    conv_weight, down_weight = arrange_weights(conv_weight, down_weight)
    own, buf = prep(features[0, 0, 0], boundary_rows[0, 0])
    left, right = neighbours("gx", buf)
    line = jnp.stack([left, buf, right])
    low, high = neighbours("gy", line)
    mid = jnp.stack([low, line, high], axis=1).reshape(9, BND // 2, 128)
    far = lax.ppermute(mid, "gz", [(0, 1), (1, 0)])
    place = lax.axis_index("gz").astype(jnp.int32).reshape(1)
    fine, rows = conv(
        place,
        own,
        mid,
        far,
        in_maps[0, 0, 0].reshape(STEPS, 2, 2, BLOCKS, 128),
        out_maps[0, 0, 0].reshape(STEPS, 2, 2, BLOCKS, 128),
        conv_weight,
        scale_one[None],
        shift_one[None],
    )
    coarse = None
    for chunk in range(CHUNKS):
        packed = pack(rows, send_rows[0, 0, 0], chunk)
        arrived = lax.all_to_all(packed, "gx", split_axis=0, concat_axis=0, tiled=True)
        coarse = down(
            chunk, arrived, recv_coarse[0, 0, 0], down_weight, coarse, scale_two[None], shift_two[None]
        )
    return (fine[None, None, None], coarse[None, None, None])


def solution(mesh):
    return jax.shard_map(
        body,
        mesh=mesh,
        in_specs=(
            P("gx", "gy", "gz", None, None),
            P("gx", "gy", "gz", None),
            P("gx", "gy", "gz", None, None),
            P("gx", "gy", "gz", None, None),
            P("gx", "gy", "gz", None, None),
            P("gx", "gy", "gz", None, None),
            P(),
            P(),
            P(),
            P(),
            P(),
            P(),
        ),
        out_specs=(P("gx", "gy", "gz", None, None), P("gx", "gy", "gz", None, None)),
        check_vma=False,
    )
```

```python
import functools

import jax
import jax.numpy as jnp
from jax import lax
from jax.experimental import pallas as pl
from jax.experimental.pallas import tpu as pltpu
from jax.sharding import PartitionSpec as P

CH = 64
CHO = 128
VOX = 6144
PAIRS = 3072
BND = 512
COARSE = 3072
OWNERS = 32
CAP = 384
ZERO_ROW = VOX + 27 * BND
TABLE = ZERO_ROW + 8
ROWS = VOX + 8
TILE = 256
TILES = VOX // TILE
BLOCK = 1024
BLOCKS = VOX // BLOCK
CUTS = PAIRS // (128 * BLOCKS)
STEPS = 13
GROUP = 48
HALF = CAP // 2
ACCS = 8
CHUNKS = ((0, 3), (3, 1))
F32 = jnp.float32
BF16 = jnp.bfloat16
MIB = 1 << 20

VMEM = pl.BlockSpec(memory_space=pltpu.VMEM)
SMEM = pl.BlockSpec(memory_space=pltpu.SMEM)
ANY = pl.BlockSpec(memory_space=pl.ANY)


def params(mib):
    return pltpu.CompilerParams(vmem_limit_bytes=mib * MIB)


def low_lanes(rows=1):
    return lax.broadcasted_iota(jnp.int32, (rows, 128), 1) < CH


def split(x):
    hi = x.astype(BF16)
    lo = (x - hi.astype(F32)).astype(BF16)
    return hi, lo


PIECE = VOX // 4


def prep_kernel(own_ref, rows_ref, table_out_ref, buf_ref, x_ref, table_ref, in_sem, out_sem):
    arriving, leaving = [], []
    for i in range(4):
        at = pl.ds(i * PIECE, PIECE)
        arriving.append(pltpu.make_async_copy(own_ref.at[:, at], x_ref.at[:, at], in_sem.at[i]))
        leaving.append(
            pltpu.make_async_copy(table_ref.at[at, :], table_out_ref.at[at, :], out_sem.at[i])
        )
    for copy in arriving:
        copy.start()
    for i in range(4):
        arriving[i].wait()

        def turn(t, carry):
            at = pl.ds(pl.multiple_of(i * PIECE + t * TILE, TILE), TILE)
            x = x_ref[:, at]
            table_ref[at, :] = jnp.concatenate([x, x], axis=0).T
            return carry

        lax.fori_loop(0, PIECE // TILE, turn, 0)
        leaving[i].start()
    low = low_lanes()

    def pick(i, carry):
        for u in range(32):
            r = i * 32 + u
            first = table_ref[pl.ds(rows_ref[0, r], 1), :]
            second = table_ref[pl.ds(rows_ref[0, r + BND // 2], 1), :]
            buf_ref[pl.ds(r, 1), :] = jnp.where(low, first, second)
        return carry

    lax.fori_loop(0, BND // 64, pick, 0)
    for copy in leaving:
        copy.wait()


def prep(own, rows):
    return pl.pallas_call(
        prep_kernel,
        out_shape=(
            jax.ShapeDtypeStruct((VOX, 128), F32),
            jax.ShapeDtypeStruct((BND // 2, 128), F32),
        ),
        in_specs=[ANY, SMEM],
        out_specs=(ANY, VMEM),
        scratch_shapes=[
            pltpu.VMEM((CH, VOX), F32),
            pltpu.VMEM((VOX, 128), F32),
            pltpu.SemaphoreType.DMA((4,)),
            pltpu.SemaphoreType.DMA((4,)),
        ],
        compiler_params=params(60),
        name="prep",
    )(own, rows)


def spread(s_ref, start, buf):
    other = pltpu.roll(buf, CH, 1)
    low = low_lanes(BND // 2)
    s_ref[pl.ds(start, BND // 2), :] = jnp.where(low, buf, other)
    s_ref[pl.ds(start + BND // 2, BND // 2), :] = jnp.where(low, other, buf)


TABLES = 4
SPLIT = OWNERS // TABLES
SLOT_SCRATCH = [pltpu.SemaphoreType.DMA((TABLES,))] + [
    pltpu.SMEM((SPLIT, CAP // 128, 128), jnp.int32)
] * TABLES


def slot_tables(table_ref, sem, refs):
    return [
        pltpu.make_async_copy(table_ref.at[i], ref, sem.at[i]) for i, ref in enumerate(refs)
    ]


def in_quarters(table):
    return table.reshape(TABLES, SPLIT, CAP // 128, 128)


def pack_rows(chunk, rows_ref, refs, out_ref):
    start, groups = chunk
    low = low_lanes()

    def owner(a, carry):
        for u in range(groups * GROUP):
            r = start * GROUP + u
            for part, ref in enumerate(refs):
                first, second = (
                    rows_ref[pl.ds(ref[a, t // 128, t % 128], 1), :] for t in (r, r + HALF)
                )
                out_ref[a + part * SPLIT, pl.ds(u, 1), :] = jnp.where(low, first, second)
        return carry

    lax.fori_loop(0, SPLIT, owner, 0)


def conv_kernel(
    place_ref, own_ref, mid_in_ref, far_in_ref, ins_ref, outs_ref, w_in_ref, norm_ref,
    table_ref, fine_out_ref, rows_out_ref, packed_out_ref,
    s_ref, g0_ref, g1_ref, acc_ref, fine_ref, packed_ref, mid_ref, far_ref, w_ref, in_sem, out_sem, list_sem, *refs,
):
    list_refs, slot_sem, slot_refs = refs[: 4 * CUTS], refs[4 * CUTS], refs[4 * CUTS + 1 :]
    slot_copies = slot_tables(table_ref, slot_sem, slot_refs)
    for copy in slot_copies:
        copy.start()
    mid_copy, far_copy, own_copy, w_copy = (
        pltpu.make_async_copy(source, target, in_sem.at[i])
        for i, (source, target) in enumerate(
            (
                (mid_in_ref, mid_ref),
                (far_in_ref, far_ref),
                (own_ref, s_ref.at[pl.ds(0, VOX), :]),
                (w_in_ref, w_ref),
            )
        )
    )
    for copy in (mid_copy, far_copy, own_copy, w_copy):
        copy.start()

    def lists(s, slot):
        return [
            pltpu.make_async_copy(
                (ins_ref, outs_ref)[i // (2 * CUTS)].at[s, i // CUTS % 2, i % CUTS],
                ref.at[slot],
                list_sem.at[slot, i],
            )
            for i, ref in enumerate(list_refs)
        ]

    for copy in lists(0, 0):
        copy.start()
    def clear(t, carry):
        at = pl.ds(pl.multiple_of(t * TILE, TILE), TILE)
        g0_ref[at, :] = jnp.zeros((TILE, 128), F32)
        acc_ref[at, :] = jnp.zeros((TILE, 128), F32)
        return carry

    lax.fori_loop(0, TILES, clear, 0)
    mid_copy.wait()
    far_copy.wait()
    here = place_ref[0]
    other = 2 - 2 * here
    same = 2 * here
    empty = jnp.zeros((BND, 128), F32)

    def fill(e, carry):
        base = VOX + e * 3 * BND
        spread(s_ref, pl.multiple_of(base + BND, BND), mid_ref[e])
        spread(s_ref, pl.multiple_of(base + other * BND, BND), far_ref[e])
        s_ref[pl.ds(pl.multiple_of(base + same * BND, BND), BND), :] = empty
        return carry

    lax.fori_loop(0, 9, fill, 0)
    s_ref[pl.ds(ZERO_ROW, 8), :] = jnp.zeros((8, 128), F32)

    low = low_lanes()
    high = jnp.logical_not(low)
    own_copy.wait()

    def centre(t, carry):
        at = pl.ds(pl.multiple_of(t * TILE, TILE), TILE)
        g1_ref[at, :] = s_ref[at, :]
        return carry

    lax.fori_loop(0, TILES, centre, 0)
    w_copy.wait()

    def product(ref, at, s):
        hi, lo = split(ref[at, :])
        return jnp.dot(
            jnp.concatenate([hi, lo], axis=1), w_ref[s], preferred_element_type=F32
        )

    def phase(s, slot, now_ref, last_ref, more):
        for copy in lists(s, slot):
            copy.wait()
        if more:
            for copy in lists(s + 1, 1 - slot):
                copy.start()

        def body(t, carry):
            at = pl.ds(pl.multiple_of(t * BLOCK, BLOCK), BLOCK)
            acc_ref[at, :] += product(last_ref, at, s)
            last_ref[at, :] = jnp.zeros((BLOCK, 128), F32)
            for u in range(128):
                for i in range(2 * CUTS):
                    row = s_ref[pl.ds(list_refs[i][slot, t, u], 1), :]
                    pltpu.store(
                        now_ref.at[pl.ds(list_refs[i + 2 * CUTS][slot, t, u], 1), :],
                        row,
                        mask=(low, high)[i // CUTS],
                    )
            return carry

        lax.fori_loop(0, BLOCKS, body, 0)

    def two(i, carry):
        phase(2 * i, 0, g0_ref, g1_ref, True)
        phase(2 * i + 1, 1, g1_ref, g0_ref, True)
        return carry

    lax.fori_loop(0, (STEPS - 1) // 2, two, 0)
    phase(STEPS - 1, 0, g0_ref, g1_ref, False)
    low_tile = low_lanes(128)
    scale, shift = norm_ref[0:1, :], norm_ref[1:2, :]

    def finish(t, carry):
        at = pl.ds(pl.multiple_of(t * TILE, TILE), TILE)
        total = acc_ref[at, :] + product(g0_ref, at, STEPS)
        total = total + pltpu.roll(total, CH, 1)
        fine = jnp.maximum(scale * total + shift, 0.0)
        acc_ref[at, :] = fine
        turned = jnp.where(low_tile, fine[:128], fine[128:]).T
        fine_ref[:, pl.ds(pl.multiple_of(t * TILE, TILE), 128)] = turned[:CH]
        fine_ref[:, pl.ds(pl.multiple_of(t * TILE + 128, 128), 128)] = turned[CH:]
        return carry

    lax.fori_loop(0, TILES, finish, 0)
    acc_ref[pl.ds(VOX, 8), :] = jnp.zeros((8, 128), F32)
    outgoing = [
        pltpu.make_async_copy(acc_ref, rows_out_ref, out_sem.at[0]),
        pltpu.make_async_copy(fine_ref, fine_out_ref, out_sem.at[1]),
    ]
    for copy in slot_copies:
        copy.wait()
    for copy in outgoing:
        copy.start()
    pack_rows(CHUNKS[0], acc_ref, slot_refs, packed_ref)
    packed = pltpu.make_async_copy(packed_ref, packed_out_ref, out_sem.at[2])
    packed.start()
    for copy in (*outgoing, packed):
        copy.wait()


def conv(place, own, mid, far, ins, outs, weights, norm, table):
    packed = (OWNERS, CHUNKS[0][1] * GROUP, 128)
    return pl.pallas_call(
        conv_kernel,
        out_shape=(
            jax.ShapeDtypeStruct((CH, VOX), F32),
            jax.ShapeDtypeStruct((ROWS, 128), F32),
            jax.ShapeDtypeStruct(packed, F32),
        ),
        in_specs=[SMEM, ANY, ANY, ANY, ANY, ANY, ANY, VMEM, ANY],
        out_specs=(ANY, ANY, ANY),
        scratch_shapes=[
            pltpu.VMEM((TABLE, 128), F32),
            pltpu.VMEM((ROWS, 128), F32),
            pltpu.VMEM((ROWS, 128), F32),
            pltpu.VMEM((ROWS, 128), F32),
            pltpu.VMEM((CH, VOX), F32),
            pltpu.VMEM(packed, F32),
            pltpu.VMEM((9, BND // 2, 128), F32),
            pltpu.VMEM((9, BND // 2, 128), F32),
            pltpu.VMEM((STEPS + 1, 256, 128), BF16),
            pltpu.SemaphoreType.DMA((4,)),
            pltpu.SemaphoreType.DMA((3,)),
            pltpu.SemaphoreType.DMA((2, 4 * CUTS)),
        ]
        + [pltpu.SMEM((2, BLOCKS, 128), jnp.int32)] * (4 * CUTS)
        + SLOT_SCRATCH,
        compiler_params=params(60),
        name="conv",
    )(place, own, mid, far, ins, outs, weights, norm, table)


def pack_kernel(chunk, rows_ref, table_ref, out_ref, sem, *refs):
    copies = slot_tables(table_ref, sem, refs)
    for copy in copies:
        copy.start()
    for copy in copies:
        copy.wait()
    pack_rows(chunk, rows_ref, refs, out_ref)


def pack(rows, table, chunk):
    return pl.pallas_call(
        functools.partial(pack_kernel, chunk),
        out_shape=jax.ShapeDtypeStruct((OWNERS, chunk[1] * GROUP, 128), F32),
        in_specs=[VMEM, ANY],
        out_specs=VMEM,
        scratch_shapes=SLOT_SCRATCH,
        compiler_params=params(60),
        cost_estimate=pl.CostEstimate(flops=0, bytes_accessed=10 * MIB, transcendentals=0),
        name=f"pack{chunk[0]}",
    )(rows, table)


def down_kernel(chunk, first, last, *args):
    x_ref, cols_ref, w_ref, norm_ref, *rest = args
    if not first:
        before_in_ref, *rest, before_ref, before_sem = rest
        before_copy = pltpu.make_async_copy(before_in_ref, before_ref, before_sem)
        before_copy.start()
    out_ref, sem, *rest = rest
    refs, (p0_ref, p1_ref, *z_refs) = rest[:TABLES], rest[TABLES:]
    copies = slot_tables(cols_ref, sem, refs)
    for copy in copies:
        copy.start()
    start, groups = chunk

    def clear(t, carry):
        at = pl.ds(pl.multiple_of(t * 128, 128), 128)
        for z_ref in z_refs:
            z_ref[at, :] = jnp.zeros((128, 128), F32)
        return carry

    lax.fori_loop(0, COARSE // 128, clear, 0)
    for g in range(groups):

        def multiply(i, carry):
            x = x_ref[pl.ds(i * 8, 8), pl.ds(g * GROUP, GROUP), :].reshape(8 * GROUP, 128)
            hi, lo = split(x)
            part = jnp.dot(hi, w_ref[0, start + g], preferred_element_type=F32)
            part += jnp.dot(lo, w_ref[0, start + g], preferred_element_type=F32)
            part += jnp.dot(hi, w_ref[1, start + g], preferred_element_type=F32)
            at = pl.ds(pl.multiple_of((g * OWNERS + i * 8) * GROUP, 8 * GROUP), 8 * GROUP)
            p0_ref[at, :] = part[:, :128]
            p1_ref[at, :] = part[:, 128:]
            return carry

        lax.fori_loop(0, OWNERS // 8, multiply, 0)

    def source(s, carry):
        for u in range(groups * GROUP):
            group, place = divmod(u, GROUP)
            todo = []
            for i, z_ref in enumerate(z_refs):
                part, half = i % TABLES, i // TABLES
                row = (group * OWNERS + s + part * SPLIT) * GROUP + place
                t = start * GROUP + u + half * HALF
                at = pl.ds(refs[part][s, t // 128, t % 128], 1)
                todo.append((z_ref, at, z_ref[at, :] + (p0_ref, p1_ref)[half][pl.ds(row, 1), :]))
            for z_ref, at, value in todo:
                z_ref[at, :] = value
        return carry

    for copy in copies:
        copy.wait()
    lax.fori_loop(0, SPLIT, source, 0)

    if not first:
        before_copy.wait()

    def finish(t, carry):
        at = pl.ds(pl.multiple_of(t * 128, 128), 128)
        total = z_refs[0][at, :]
        for z_ref in z_refs[1:]:
            total = total + z_ref[at, :]
        if not first:
            total = total + before_ref[at, :]
        if last:
            out_ref[:, at] = jnp.maximum(norm_ref[2:3, :] * total + norm_ref[3:4, :], 0.0).T
        else:
            out_ref[at, :] = total
        return carry

    lax.fori_loop(0, COARSE // 128, finish, 0)


def down(chunk, arrived, cols, weights, norm, before):
    last = chunk == CHUNKS[-1]
    carried = [] if before is None else [before]
    return pl.pallas_call(
        functools.partial(down_kernel, chunk, before is None, last),
        out_shape=jax.ShapeDtypeStruct((CHO, COARSE) if last else (COARSE, CHO), F32),
        in_specs=[VMEM, ANY, VMEM, VMEM] + [ANY] * len(carried),
        out_specs=VMEM,
        scratch_shapes=SLOT_SCRATCH
        + [pltpu.VMEM((OWNERS * chunk[1] * GROUP, 128), F32)] * 2
        + [pltpu.VMEM((COARSE + 8, 128), F32)] * ACCS
        + [pltpu.VMEM((COARSE, CHO), F32), pltpu.SemaphoreType.DMA] * len(carried),
        compiler_params=params(60),
        cost_estimate=pl.CostEstimate(flops=0, bytes_accessed=20 * MIB, transcendentals=0),
        name=f"down{chunk[0]}",
    )(arrived, cols, weights, norm, *carried)


def neighbours(axis, block):
    count = lax.axis_size(axis)
    forward = [(i, i + 1) for i in range(count - 1)]
    backward = [(target, source) for source, target in forward]
    return lax.ppermute(block, axis, forward), lax.ppermute(block, axis, backward)


def weights_kernel(
    conv_ref, down_ref, scale_one_ref, shift_one_ref, scale_two_ref, shift_two_ref,
    conv_out_ref, down_out_ref, norm_ref,
):
    for i, ref in enumerate((scale_one_ref, shift_one_ref)):
        norm_ref[i : i + 1, :] = jnp.concatenate([ref[...]] * 2, axis=1)
    norm_ref[2:3, :] = scale_two_ref[...]
    norm_ref[3:4, :] = shift_two_ref[...]
    norm_ref[4:8, :] = jnp.zeros((4, 128), F32)
    empty = jnp.zeros((CH, 128), F32)
    for s in range(STEPS + 1):
        if s == 0:
            first, second = conv_ref[13], jnp.zeros((CH, CH), F32)
        else:
            first, second = (conv_ref[k + (k >= 13)] for k in (2 * s - 2, 2 * s - 1))
        both = jnp.concatenate([first, second], axis=1)
        hi = both.astype(BF16).astype(F32)
        top = jnp.concatenate([hi, both - hi], axis=0)
        bottom = jnp.concatenate([hi, empty], axis=0)
        conv_out_ref[s, :128, :] = top.T.astype(BF16)
        conv_out_ref[s, 128:, :] = bottom.T.astype(BF16)
    left = lax.broadcasted_iota(jnp.int32, (128, CHO), 0) < CH
    for c in range(4):
        both = jnp.concatenate([down_ref[c], down_ref[c + 4]], axis=1).T
        for i, part in enumerate(split(both)):
            part = part.astype(F32)
            down_out_ref[i, c, :, :CHO] = jnp.where(left, part, 0.0).astype(BF16)
            down_out_ref[i, c, :, CHO:] = jnp.where(left, 0.0, part).astype(BF16)


def arrange_weights(conv_weight, down_weight, *norms):
    return pl.pallas_call(
        weights_kernel,
        out_shape=(
            jax.ShapeDtypeStruct((STEPS + 1, 256, 128), BF16),
            jax.ShapeDtypeStruct((2, 4, 128, 2 * CHO), BF16),
            jax.ShapeDtypeStruct((8, 128), F32),
        ),
        in_specs=[VMEM] * 6,
        out_specs=(VMEM, VMEM, VMEM),
        compiler_params=params(60),
        cost_estimate=pl.CostEstimate(flops=0, bytes_accessed=10 * MIB, transcendentals=0),
        name="weights",
    )(conv_weight, down_weight, *norms)


def body(
    features,
    boundary_rows,
    in_maps,
    out_maps,
    send_rows,
    recv_coarse,
    conv_weight,
    scale_one,
    shift_one,
    down_weight,
    scale_two,
    shift_two,
):
    conv_weight, down_weight, norm = arrange_weights(
        conv_weight, down_weight, scale_one[None], shift_one[None], scale_two[None], shift_two[None]
    )
    own, buf = prep(features[0, 0, 0], boundary_rows[0, 0])
    left, right = neighbours("gx", buf)
    line = jnp.stack([left, buf, right])
    line, conv_weight, down_weight, norm = lax.optimization_barrier(
        (line, conv_weight, down_weight, norm)
    )
    low, high = neighbours("gy", line)
    ins, outs = (x[0, 0, 0].reshape(STEPS, 2, CUTS, BLOCKS, 128) for x in (in_maps, out_maps))
    places, cols = in_quarters(send_rows[0, 0, 0]), in_quarters(recv_coarse[0, 0, 0])
    low, high, ins, outs, places, cols = lax.optimization_barrier(
        (low, high, ins, outs, places, cols)
    )
    mid = jnp.stack([low, line, high], axis=1).reshape(9, BND // 2, 128)
    far = lax.ppermute(mid, "gz", [(0, 1), (1, 0)])
    place = lax.axis_index("gz").astype(jnp.int32).reshape(1)
    fine, rows, packed = conv(
        place,
        own,
        mid,
        far,
        ins,
        outs,
        conv_weight,
        norm,
        places,
    )
    coarse = None
    for chunk in CHUNKS:
        if chunk != CHUNKS[0]:
            packed = pack(rows, places, chunk)
        arrived = lax.all_to_all(packed, "gx", split_axis=0, concat_axis=0, tiled=True)
        coarse = down(chunk, arrived, cols, down_weight, norm, coarse)
    return (fine[None, None, None], coarse[None, None, None])


def solution(mesh):
    return jax.shard_map(
        body,
        mesh=mesh,
        in_specs=(
            P("gx", "gy", "gz", None, None),
            P("gx", "gy", "gz", None),
            P("gx", "gy", "gz", None, None),
            P("gx", "gy", "gz", None, None),
            P("gx", "gy", "gz", None, None),
            P("gx", "gy", "gz", None, None),
            P(),
            P(),
            P(),
            P(),
            P(),
            P(),
        ),
        out_specs=(P("gx", "gy", "gz", None, None), P("gx", "gy", "gz", None, None)),
        check_vma=False,
    )
```

```python
import functools

import jax
import jax.numpy as jnp
from jax import lax
from jax.experimental import pallas as pl
from jax.experimental.pallas import tpu as pltpu
from jax.sharding import PartitionSpec as P

CH = 64
CHO = 128
VOX = 6144
PAIRS = 3072
BND = 512
COARSE = 3072
OWNERS = 32
CAP = 384
ZERO_ROW = VOX + 27 * BND
TABLE = ZERO_ROW + 8
ROWS = VOX + 8
TILE = 256
TILES = VOX // TILE
BLOCK = 1024
BLOCKS = VOX // BLOCK
CUTS = PAIRS // (128 * BLOCKS)
STEPS = 13
GROUP = 48
HALF = CAP // 2
ACCS = 8
CHUNKS = ((0, 3), (3, 1))
F32 = jnp.float32
BF16 = jnp.bfloat16
MIB = 1 << 20

VMEM = pl.BlockSpec(memory_space=pltpu.VMEM)
SMEM = pl.BlockSpec(memory_space=pltpu.SMEM)
ANY = pl.BlockSpec(memory_space=pl.ANY)


def params(mib):
    return pltpu.CompilerParams(vmem_limit_bytes=mib * MIB)


def low_lanes(rows=1):
    return lax.broadcasted_iota(jnp.int32, (rows, 128), 1) < CH


def split(x):
    hi = x.astype(BF16)
    lo = (x - hi.astype(F32)).astype(BF16)
    return hi, lo


PIECE = VOX // 4


def prep_kernel(own_ref, rows_ref, table_out_ref, buf_ref, x_ref, table_ref, in_sem, out_sem):
    arriving, leaving = [], []
    for i in range(4):
        at = pl.ds(i * PIECE, PIECE)
        arriving.append(pltpu.make_async_copy(own_ref.at[:, at], x_ref.at[:, at], in_sem.at[i]))
        leaving.append(
            pltpu.make_async_copy(table_ref.at[at, :], table_out_ref.at[at, :], out_sem.at[i])
        )
    for copy in arriving:
        copy.start()
    for i in range(4):
        arriving[i].wait()

        def turn(t, carry):
            at = pl.ds(pl.multiple_of(i * PIECE + t * TILE, TILE), TILE)
            x = x_ref[:, at]
            table_ref[at, :] = jnp.concatenate([x, x], axis=0).T
            return carry

        lax.fori_loop(0, PIECE // TILE, turn, 0)
        leaving[i].start()
    low = low_lanes()

    def pick(i, carry):
        for u in range(32):
            r = i * 32 + u
            first = table_ref[pl.ds(rows_ref[0, r], 1), :]
            second = table_ref[pl.ds(rows_ref[0, r + BND // 2], 1), :]
            buf_ref[pl.ds(r, 1), :] = jnp.where(low, first, second)
        return carry

    lax.fori_loop(0, BND // 64, pick, 0)
    for copy in leaving:
        copy.wait()


def prep(own, rows):
    return pl.pallas_call(
        prep_kernel,
        out_shape=(
            jax.ShapeDtypeStruct((VOX, 128), F32),
            jax.ShapeDtypeStruct((BND // 2, 128), F32),
        ),
        in_specs=[ANY, SMEM],
        out_specs=(ANY, VMEM),
        scratch_shapes=[
            pltpu.VMEM((CH, VOX), F32),
            pltpu.VMEM((VOX, 128), F32),
            pltpu.SemaphoreType.DMA((4,)),
            pltpu.SemaphoreType.DMA((4,)),
        ],
        compiler_params=params(60),
        name="prep",
    )(own, rows)


def spread(s_ref, start, buf):
    other = pltpu.roll(buf, CH, 1)
    low = low_lanes(BND // 2)
    s_ref[pl.ds(start, BND // 2), :] = jnp.where(low, buf, other)
    s_ref[pl.ds(start + BND // 2, BND // 2), :] = jnp.where(low, other, buf)


TABLES = 4
SPLIT = OWNERS // TABLES
SLOT_SCRATCH = [pltpu.SemaphoreType.DMA((TABLES,))] + [
    pltpu.SMEM((SPLIT, CAP // 128, 128), jnp.int32)
] * TABLES


def slot_tables(table_ref, sem, refs):
    return [
        pltpu.make_async_copy(table_ref.at[i], ref, sem.at[i]) for i, ref in enumerate(refs)
    ]


def in_quarters(table):
    return table.reshape(TABLES, SPLIT, CAP // 128, 128)


def pack_rows(chunk, rows_ref, refs, out_ref, low_owner=0, high_owner=SPLIT):
    start, groups = chunk
    low = low_lanes()

    def owner(a, carry):
        for u in range(groups * GROUP):
            r = start * GROUP + u
            for part, ref in enumerate(refs):
                first, second = (
                    rows_ref[pl.ds(ref[a, t // 128, t % 128], 1), :] for t in (r, r + HALF)
                )
                out_ref[a + part * SPLIT, pl.ds(u, 1), :] = jnp.where(low, first, second)
        return carry

    lax.fori_loop(low_owner, high_owner, owner, 0)


def conv_kernel(
    place_ref, own_ref, mid_in_ref, far_in_ref, ins_ref, outs_ref, w_in_ref, norm_ref,
    table_ref, fine_out_ref, rows_out_ref, packed_out_ref,
    s_ref, g0_ref, g1_ref, acc_ref, fine_ref, packed_ref, mid_ref, far_ref, w_ref, in_sem, out_sem, list_sem, *refs,
):
    list_refs, slot_sem, slot_refs = refs[: 4 * CUTS], refs[4 * CUTS], refs[4 * CUTS + 1 :]
    slot_copies = slot_tables(table_ref, slot_sem, slot_refs)
    for copy in slot_copies:
        copy.start()
    mid_copy, far_copy, own_copy, w_copy = (
        pltpu.make_async_copy(source, target, in_sem.at[i])
        for i, (source, target) in enumerate(
            (
                (mid_in_ref, mid_ref),
                (far_in_ref, far_ref),
                (own_ref, s_ref.at[pl.ds(0, VOX), :]),
                (w_in_ref, w_ref),
            )
        )
    )
    for copy in (mid_copy, far_copy, own_copy, w_copy):
        copy.start()

    def lists(s, slot):
        return [
            pltpu.make_async_copy(
                (ins_ref, outs_ref)[i // (2 * CUTS)].at[s, i // CUTS % 2, i % CUTS],
                ref.at[slot],
                list_sem.at[slot, i],
            )
            for i, ref in enumerate(list_refs)
        ]

    for copy in lists(0, 0):
        copy.start()
    def clear(t, carry):
        at = pl.ds(pl.multiple_of(t * TILE, TILE), TILE)
        g0_ref[at, :] = jnp.zeros((TILE, 128), F32)
        acc_ref[at, :] = jnp.zeros((TILE, 128), F32)
        return carry

    lax.fori_loop(0, TILES, clear, 0)
    mid_copy.wait()
    far_copy.wait()
    here = place_ref[0]
    other = 2 - 2 * here
    same = 2 * here
    empty = jnp.zeros((BND, 128), F32)

    def fill(e, carry):
        base = VOX + e * 3 * BND
        spread(s_ref, pl.multiple_of(base + BND, BND), mid_ref[e])
        spread(s_ref, pl.multiple_of(base + other * BND, BND), far_ref[e])
        s_ref[pl.ds(pl.multiple_of(base + same * BND, BND), BND), :] = empty
        return carry

    lax.fori_loop(0, 9, fill, 0)
    s_ref[pl.ds(ZERO_ROW, 8), :] = jnp.zeros((8, 128), F32)

    low = low_lanes()
    high = jnp.logical_not(low)
    own_copy.wait()

    def centre(t, carry):
        at = pl.ds(pl.multiple_of(t * TILE, TILE), TILE)
        g1_ref[at, :] = s_ref[at, :]
        return carry

    lax.fori_loop(0, TILES, centre, 0)
    w_copy.wait()

    def product(ref, at, s):
        hi, lo = split(ref[at, :])
        return jnp.dot(
            jnp.concatenate([hi, lo], axis=1), w_ref[s], preferred_element_type=F32
        )

    def phase(s, slot, now_ref, last_ref, more):
        for copy in lists(s, slot):
            copy.wait()
        if more:
            for copy in lists(s + 1, 1 - slot):
                copy.start()

        def body(t, carry):
            at = pl.ds(pl.multiple_of(t * BLOCK, BLOCK), BLOCK)
            acc_ref[at, :] += product(last_ref, at, s)
            last_ref[at, :] = jnp.zeros((BLOCK, 128), F32)
            for u in range(128):
                for i in range(2 * CUTS):
                    row = s_ref[pl.ds(list_refs[i][slot, t, u], 1), :]
                    pltpu.store(
                        now_ref.at[pl.ds(list_refs[i + 2 * CUTS][slot, t, u], 1), :],
                        row,
                        mask=(low, high)[i // CUTS],
                    )
            return carry

        lax.fori_loop(0, BLOCKS, body, 0)

    def two(i, carry):
        phase(2 * i, 0, g0_ref, g1_ref, True)
        phase(2 * i + 1, 1, g1_ref, g0_ref, True)
        return carry

    lax.fori_loop(0, (STEPS - 1) // 2, two, 0)
    phase(STEPS - 1, 0, g0_ref, g1_ref, False)
    low_tile = low_lanes(128)
    scale, shift = norm_ref[0:1, :], norm_ref[1:2, :]

    def finish(t, carry):
        at = pl.ds(pl.multiple_of(t * TILE, TILE), TILE)
        total = acc_ref[at, :] + product(g0_ref, at, STEPS)
        total = total + pltpu.roll(total, CH, 1)
        fine = jnp.maximum(scale * total + shift, 0.0)
        acc_ref[at, :] = fine
        turned = jnp.where(low_tile, fine[:128], fine[128:]).T
        fine_ref[:, pl.ds(pl.multiple_of(t * TILE, TILE), 128)] = turned[:CH]
        fine_ref[:, pl.ds(pl.multiple_of(t * TILE + 128, 128), 128)] = turned[CH:]
        return carry

    lax.fori_loop(0, TILES, finish, 0)
    acc_ref[pl.ds(VOX, 8), :] = jnp.zeros((8, 128), F32)
    outgoing = [
        pltpu.make_async_copy(acc_ref, rows_out_ref, out_sem.at[0]),
        pltpu.make_async_copy(fine_ref, fine_out_ref, out_sem.at[1]),
    ]
    for copy in slot_copies:
        copy.wait()
    for copy in outgoing:
        copy.start()
    for i in range(2):
        low_owner, high_owner = i * SPLIT // 2, (i + 1) * SPLIT // 2
        pack_rows(CHUNKS[0], acc_ref, slot_refs, packed_ref, low_owner, high_owner)
        for part in range(TABLES):
            at = pl.ds(part * SPLIT + low_owner, SPLIT // 2)
            outgoing.append(
                pltpu.make_async_copy(
                    packed_ref.at[at], packed_out_ref.at[at], out_sem.at[2 + i * TABLES + part]
                )
            )
            outgoing[-1].start()
    for copy in outgoing:
        copy.wait()


def conv(place, own, mid, far, ins, outs, weights, norm, table):
    packed = (OWNERS, CHUNKS[0][1] * GROUP, 128)
    return pl.pallas_call(
        conv_kernel,
        out_shape=(
            jax.ShapeDtypeStruct((CH, VOX), F32),
            jax.ShapeDtypeStruct((ROWS, 128), F32),
            jax.ShapeDtypeStruct(packed, F32),
        ),
        in_specs=[SMEM, ANY, ANY, ANY, ANY, ANY, ANY, VMEM, ANY],
        out_specs=(ANY, ANY, ANY),
        scratch_shapes=[
            pltpu.VMEM((TABLE, 128), F32),
            pltpu.VMEM((ROWS, 128), F32),
            pltpu.VMEM((ROWS, 128), F32),
            pltpu.VMEM((ROWS, 128), F32),
            pltpu.VMEM((CH, VOX), F32),
            pltpu.VMEM(packed, F32),
            pltpu.VMEM((9, BND // 2, 128), F32),
            pltpu.VMEM((9, BND // 2, 128), F32),
            pltpu.VMEM((STEPS + 1, 256, 128), BF16),
            pltpu.SemaphoreType.DMA((4,)),
            pltpu.SemaphoreType.DMA((2 + 2 * TABLES,)),
            pltpu.SemaphoreType.DMA((2, 4 * CUTS)),
        ]
        + [pltpu.SMEM((2, BLOCKS, 128), jnp.int32)] * (4 * CUTS)
        + SLOT_SCRATCH,
        compiler_params=params(60),
        name="conv",
    )(place, own, mid, far, ins, outs, weights, norm, table)


def pack_kernel(chunk, rows_ref, table_ref, out_ref, sem, *refs):
    copies = slot_tables(table_ref, sem, refs)
    for copy in copies:
        copy.start()
    for copy in copies:
        copy.wait()
    pack_rows(chunk, rows_ref, refs, out_ref)


def pack(rows, table, chunk):
    return pl.pallas_call(
        functools.partial(pack_kernel, chunk),
        out_shape=jax.ShapeDtypeStruct((OWNERS, chunk[1] * GROUP, 128), F32),
        in_specs=[VMEM, ANY],
        out_specs=VMEM,
        scratch_shapes=SLOT_SCRATCH,
        compiler_params=params(60),
        cost_estimate=pl.CostEstimate(flops=0, bytes_accessed=10 * MIB, transcendentals=0),
        name=f"pack{chunk[0]}",
    )(rows, table)


def down_kernel(chunk, first, last, *args):
    x_in_ref, cols_ref, w_in_ref, norm_ref, *rest = args
    if not first:
        before_in_ref, *rest, before_ref, before_sem = rest
        before_copy = pltpu.make_async_copy(before_in_ref, before_ref, before_sem)
        before_copy.start()
    out_ref, sem, *rest = rest
    refs, rest = rest[:TABLES], rest[TABLES:]
    x_ref, w_ref, result_ref, in_sem, out_sem, p0_ref, p1_ref, *z_refs = rest
    copies = slot_tables(cols_ref, sem, refs)
    for copy in copies:
        copy.start()
    start, groups = chunk
    x_copy = pltpu.make_async_copy(x_in_ref, x_ref, in_sem.at[0])
    w_copy = pltpu.make_async_copy(w_in_ref.at[:, pl.ds(start, groups)], w_ref, in_sem.at[1])
    x_copy.start()
    w_copy.start()

    def clear(t, carry):
        at = pl.ds(pl.multiple_of(t * 128, 128), 128)
        for z_ref in z_refs:
            z_ref[at, :] = jnp.zeros((128, 128), F32)
        return carry

    lax.fori_loop(0, COARSE // 128, clear, 0)
    x_copy.wait()
    w_copy.wait()
    for g in range(groups):

        def multiply(i, carry):
            x = x_ref[pl.ds(i * 8, 8), pl.ds(g * GROUP, GROUP), :].reshape(8 * GROUP, 128)
            hi, lo = split(x)
            part = jnp.dot(hi, w_ref[0, g], preferred_element_type=F32)
            part += jnp.dot(lo, w_ref[0, g], preferred_element_type=F32)
            part += jnp.dot(hi, w_ref[1, g], preferred_element_type=F32)
            at = pl.ds(pl.multiple_of((g * OWNERS + i * 8) * GROUP, 8 * GROUP), 8 * GROUP)
            p0_ref[at, :] = part[:, :128]
            p1_ref[at, :] = part[:, 128:]
            return carry

        lax.fori_loop(0, OWNERS // 8, multiply, 0)

    def source(s, carry):
        for u in range(groups * GROUP):
            group, place = divmod(u, GROUP)
            todo = []
            for i, z_ref in enumerate(z_refs):
                part, half = i % TABLES, i // TABLES
                row = (group * OWNERS + s + part * SPLIT) * GROUP + place
                t = start * GROUP + u + half * HALF
                at = pl.ds(refs[part][s, t // 128, t % 128], 1)
                todo.append((z_ref, at, z_ref[at, :] + (p0_ref, p1_ref)[half][pl.ds(row, 1), :]))
            for z_ref, at, value in todo:
                z_ref[at, :] = value
        return carry

    for copy in copies:
        copy.wait()
    lax.fori_loop(0, SPLIT, source, 0)

    if not first:
        before_copy.wait()

    def finish(t, carry):
        at = pl.ds(pl.multiple_of(t * 128, 128), 128)
        total = z_refs[0][at, :]
        for z_ref in z_refs[1:]:
            total = total + z_ref[at, :]
        if not first:
            total = total + before_ref[at, :]
        if last:
            result_ref[:, at] = jnp.maximum(norm_ref[2:3, :] * total + norm_ref[3:4, :], 0.0).T
        else:
            result_ref[at, :] = total
        return carry

    leaving = []
    for i in range(4):
        lax.fori_loop(i * COARSE // 512, (i + 1) * COARSE // 512, finish, 0)
        piece = pl.ds(i * COARSE // 4, COARSE // 4)
        at = (slice(None), piece) if last else (piece, slice(None))
        leaving.append(pltpu.make_async_copy(result_ref.at[at], out_ref.at[at], out_sem.at[i]))
        leaving[i].start()
    for copy in leaving:
        copy.wait()


def down(chunk, arrived, cols, weights, norm, before):
    last = chunk == CHUNKS[-1]
    carried = [] if before is None else [before]
    return pl.pallas_call(
        functools.partial(down_kernel, chunk, before is None, last),
        out_shape=jax.ShapeDtypeStruct((CHO, COARSE) if last else (COARSE, CHO), F32),
        in_specs=[ANY, ANY, ANY, VMEM] + [ANY] * len(carried),
        out_specs=ANY,
        scratch_shapes=SLOT_SCRATCH
        + [
            pltpu.VMEM((OWNERS, chunk[1] * GROUP, 128), F32),
            pltpu.VMEM((2, chunk[1], 128, 2 * CHO), BF16),
            pltpu.VMEM((CHO, COARSE) if last else (COARSE, CHO), F32),
            pltpu.SemaphoreType.DMA((2,)),
            pltpu.SemaphoreType.DMA((4,)),
        ]
        + [pltpu.VMEM((OWNERS * chunk[1] * GROUP, 128), F32)] * 2
        + [pltpu.VMEM((COARSE + 8, 128), F32)] * ACCS
        + [pltpu.VMEM((COARSE, CHO), F32), pltpu.SemaphoreType.DMA] * len(carried),
        compiler_params=params(60),
        cost_estimate=pl.CostEstimate(flops=0, bytes_accessed=20 * MIB, transcendentals=0),
        name=f"down{chunk[0]}",
    )(arrived, cols, weights, norm, *carried)


def neighbours(axis, block):
    count = lax.axis_size(axis)
    forward = [(i, i + 1) for i in range(count - 1)]
    backward = [(target, source) for source, target in forward]
    return lax.ppermute(block, axis, forward), lax.ppermute(block, axis, backward)


def weights_kernel(
    conv_ref, down_ref, scale_one_ref, shift_one_ref, scale_two_ref, shift_two_ref,
    conv_out_ref, down_out_ref, norm_ref,
):
    for i, ref in enumerate((scale_one_ref, shift_one_ref)):
        norm_ref[i : i + 1, :] = jnp.concatenate([ref[...]] * 2, axis=1)
    norm_ref[2:3, :] = scale_two_ref[...]
    norm_ref[3:4, :] = shift_two_ref[...]
    norm_ref[4:8, :] = jnp.zeros((4, 128), F32)
    empty = jnp.zeros((CH, 128), F32)
    for s in range(STEPS + 1):
        if s == 0:
            first, second = conv_ref[13], jnp.zeros((CH, CH), F32)
        else:
            first, second = (conv_ref[k + (k >= 13)] for k in (2 * s - 2, 2 * s - 1))
        both = jnp.concatenate([first, second], axis=1)
        hi = both.astype(BF16).astype(F32)
        top = jnp.concatenate([hi, both - hi], axis=0)
        bottom = jnp.concatenate([hi, empty], axis=0)
        conv_out_ref[s, :128, :] = top.T.astype(BF16)
        conv_out_ref[s, 128:, :] = bottom.T.astype(BF16)
    left = lax.broadcasted_iota(jnp.int32, (128, CHO), 0) < CH
    for c in range(4):
        both = jnp.concatenate([down_ref[c], down_ref[c + 4]], axis=1).T
        for i, part in enumerate(split(both)):
            part = part.astype(F32)
            down_out_ref[i, c, :, :CHO] = jnp.where(left, part, 0.0).astype(BF16)
            down_out_ref[i, c, :, CHO:] = jnp.where(left, 0.0, part).astype(BF16)


def arrange_weights(conv_weight, down_weight, *norms):
    return pl.pallas_call(
        weights_kernel,
        out_shape=(
            jax.ShapeDtypeStruct((STEPS + 1, 256, 128), BF16),
            jax.ShapeDtypeStruct((2, 4, 128, 2 * CHO), BF16),
            jax.ShapeDtypeStruct((8, 128), F32),
        ),
        in_specs=[VMEM] * 6,
        out_specs=(VMEM, VMEM, VMEM),
        compiler_params=params(60),
        cost_estimate=pl.CostEstimate(flops=0, bytes_accessed=10 * MIB, transcendentals=0),
        name="weights",
    )(conv_weight, down_weight, *norms)


def body(
    features,
    boundary_rows,
    in_maps,
    out_maps,
    send_rows,
    recv_coarse,
    conv_weight,
    scale_one,
    shift_one,
    down_weight,
    scale_two,
    shift_two,
):
    conv_weight, down_weight, norm = arrange_weights(
        conv_weight, down_weight, scale_one[None], shift_one[None], scale_two[None], shift_two[None]
    )
    own, buf = prep(features[0, 0, 0], boundary_rows[0, 0])
    left, right = neighbours("gx", buf)
    line = jnp.stack([left, buf, right])
    line, conv_weight, down_weight, norm = lax.optimization_barrier(
        (line, conv_weight, down_weight, norm)
    )
    low, high = neighbours("gy", line)
    ins, outs = (x[0, 0, 0].reshape(STEPS, 2, CUTS, BLOCKS, 128) for x in (in_maps, out_maps))
    places, cols = in_quarters(send_rows[0, 0, 0]), in_quarters(recv_coarse[0, 0, 0])
    low, high, ins, outs, places, cols = lax.optimization_barrier(
        (low, high, ins, outs, places, cols)
    )
    mid = jnp.stack([low, line, high], axis=1).reshape(9, BND // 2, 128)
    far = lax.ppermute(mid, "gz", [(0, 1), (1, 0)])
    place = lax.axis_index("gz").astype(jnp.int32).reshape(1)
    fine, rows, packed = conv(
        place,
        own,
        mid,
        far,
        ins,
        outs,
        conv_weight,
        norm,
        places,
    )
    coarse = None
    for chunk in CHUNKS:
        if chunk != CHUNKS[0]:
            packed = pack(rows, places, chunk)
        arrived = lax.all_to_all(packed, "gx", split_axis=0, concat_axis=0, tiled=True)
        coarse = down(chunk, arrived, cols, down_weight, norm, coarse)
    return (fine[None, None, None], coarse[None, None, None])


def solution(mesh):
    return jax.shard_map(
        body,
        mesh=mesh,
        in_specs=(
            P("gx", "gy", "gz", None, None),
            P("gx", "gy", "gz", None),
            P("gx", "gy", "gz", None, None),
            P("gx", "gy", "gz", None, None),
            P("gx", "gy", "gz", None, None),
            P("gx", "gy", "gz", None, None),
            P(),
            P(),
            P(),
            P(),
            P(),
            P(),
        ),
        out_specs=(P("gx", "gy", "gz", None, None), P("gx", "gy", "gz", None, None)),
        check_vma=False,
    )
```
